256 devices in a mesh: site: 64 (over x_lo, z, y), mode: 4 (over x_hi, core).
Axes of the slice: x: 4 (x_hi: 2, x_lo: 2; x = x_hi * 2 + x_lo), y: 4, z: 8, core: 2. Of those that a mesh axis runs over, the one named last changes fastest.
Arguments:
- basis: bfloat16 [512, 400, 512], P('site', 'mode'), may hold values from -6 to 6
- images: bfloat16 [512, 400, 496], P('site', 'mode'), may hold values from -6 to 6
- hops: bfloat16 [512, 9, 400, 400], P('site', None, 'mode'), may hold values from -0.09375 to 0.09375
- neighbours: int32 [512, 8], P('site'), may hold values from 0 to 47, as said below
- rotation: bfloat16 [512, 512], replicated, may hold values from -0.25 to 0.25
Outputs:
- projected: float32 [512, 512], replicated
- rotated_basis: bfloat16 [512, 400, 512], P('site', 'mode')
- rotated_images: bfloat16 [512, 400, 512], P('site', 'mode')
The draws below stay inside these ranges and needn't reach their ends.
Inputs may be any that keep to these rules, and one draw needn't show every extreme that they name: `neighbours`: the blocks form a periodic 4 x 4 x 4 x 512/64 lattice. Group s = 8 t + 4 gx + 2 gy + gz holds the 2 x 2 x 2 cube of time slice t at spatial offsets 2 gx, 2 gy, 2 gz, stored in its own order. Columns 0, 1, 2 name the neighbour along x, y, z forward, columns 3, 4, 5 backward, column 6 the next time slice, column 7 the previous one, each as k * 8 + q with k and q as in the reference program.
All inputs are finite; a program needn't handle non-finite values.
Results may differ from the reference program's by a relative error of at most 0.0026.
Values may be sent and summed in bfloat16 or wider, within the bound.
A program may use at most 64 MiB of HBM per device.

```python
import math
import jax
import jax.numpy as jnp

COARSE = 400
NVEC = 512
BLOCK = 16
HOPS = 9
NB_DEV = 8
OLD = 496
NBLK = 512
N_SITE = 64


def draw_neighbours(key, part):
    groups = NBLK // NB_DEV
    slices = groups // 8
    keys = jax.random.split(jax.random.fold_in(key, 17), groups)
    layout = jax.vmap(lambda k: jax.random.permutation(k, NB_DEV))(keys).astype(jnp.int32)
    inverse = jnp.argsort(layout, axis=1).astype(jnp.int32)
    group = jnp.arange(groups, dtype=jnp.int32)
    tslice = group // 8
    rest = group % 8
    ahead = (tslice + 1) % slices * 8 + rest
    behind = (tslice + slices - 1) % slices * 8 + rest
    forward_cols = []
    backward_cols = []
    for bit, piece in ((2, 1), (1, 2), (0, 3)):
        local_bit = jnp.bitwise_and(jnp.right_shift(layout, bit), 1)
        other = jnp.bitwise_xor(group, 1 << bit)
        flipped = jnp.bitwise_xor(layout, jnp.int32(1 << bit))
        pos_own = jnp.take_along_axis(inverse, flipped, axis=1)
        pos_other = inverse[other[:, None], flipped]
        fwd = jnp.where(local_bit == 0, pos_own, piece * NB_DEV + pos_other)
        bwd = jnp.where(local_bit == 1, pos_own, piece * NB_DEV + pos_other)
        forward_cols.append(fwd)
        backward_cols.append(bwd)
    next_col = 4 * NB_DEV + inverse[ahead[:, None], layout]
    prev_col = 5 * NB_DEV + inverse[behind[:, None], layout]
    table = jnp.stack(forward_cols + backward_cols + [next_col, prev_col], axis=2)
    return table.reshape(NBLK, 8).astype(jnp.int32)


def shard_levels(key, shape, cuts, least, top_value):
    def one(dim, parts):
        draws = jax.random.uniform(jax.random.fold_in(jax.random.fold_in(key, 6), dim), (parts,), jnp.float32, least / len(cuts), top_value / len(cuts))
        return jnp.repeat(jnp.exp(draws), shape[dim] // parts).reshape((-1,) + (1,) * (len(shape) - dim - 1))

    gain = one(*cuts[0])
    for cut in cuts[1:]:
        gain = gain * one(*cut)
    return gain


def gaussian(stream_key, shape, scale, limit, cuts=(), held_as=jnp.bfloat16):
    result = jax.random.normal(stream_key, shape, jnp.float32) * scale
    if len(cuts) > 0:
        result = shard_levels(stream_key, shape, cuts, -0.22, 0.18) * result
    return jnp.clip(result, min=-limit, max=limit).astype(held_as)


def setup_inputs(seed: int = 0) -> dict:
    streams_of = jax.random.split(jax.random.key(seed), 6)
    return {
        "basis": gaussian(streams_of[0], (NBLK, COARSE, NVEC), 1.0, 6.0, ((0, 64), (1, 4))),
        "images": gaussian(streams_of[1], (NBLK, COARSE, OLD), 1.0, 6.0, ((0, 64), (1, 4))),
        "hops": gaussian(streams_of[2], (NBLK, HOPS, COARSE, COARSE), (HOPS * COARSE) ** -0.5, 0.09375, ((0, 64), (2, 4))),
        "neighbours": draw_neighbours(jax.random.fold_in(streams_of[5], 71), 0),
        "rotation": gaussian(streams_of[4], (NVEC, NVEC), NVEC ** -0.5, 0.25),
    }


def neighbour_rows(neighbours):
    slices = N_SITE // 8
    block_rows = jnp.arange(NBLK, dtype=jnp.int32)
    group = block_rows // NB_DEV
    tslice = group // 8
    rest = group % 8
    ahead = (tslice + 1) % slices * 8 + rest
    behind = (tslice + slices - 1) % slices * 8 + rest
    candidates = jnp.stack([group, jnp.bitwise_xor(group, 4), jnp.bitwise_xor(group, 2), jnp.bitwise_xor(group, 1), ahead, behind], axis=1).astype(jnp.int32)
    columns = [block_rows]
    for direction in range(8):
        entry = neighbours[:, direction]
        source = jnp.take_along_axis(candidates, (entry // NB_DEV)[:, None].astype(jnp.int32), axis=1)[:, 0]
        columns.append((source * NB_DEV + entry % NB_DEV).astype(jnp.int32))
    return columns

def reference(basis, images, hops, neighbours, rotation):
    columns = neighbour_rows(neighbours)
    newest = basis[:, :, OLD:].astype(jnp.float32)
    total = jnp.zeros((NBLK, COARSE, BLOCK), jnp.float32)
    for direction in range(HOPS):
        matrices = hops[:, direction].astype(jnp.float32)
        total = total + jnp.einsum('boi,bik->bok', matrices, newest[columns[direction]])
    image_new = total.astype(jnp.bfloat16)
    images_all = jnp.concatenate([images, image_new], axis=2)
    flat_basis = basis.reshape(NBLK * COARSE, NVEC)
    flat_images = images_all.reshape(NBLK * COARSE, NVEC)
    norm_scale = 1.0 / math.sqrt(NBLK * COARSE)
    projected = jnp.dot(flat_basis.T, flat_images, preferred_element_type=jnp.float32) * norm_scale
    rotated_basis = jnp.dot(flat_basis, rotation, preferred_element_type=jnp.float32).astype(jnp.bfloat16)
    rotated_images = jnp.dot(flat_images, rotation, preferred_element_type=jnp.float32).astype(jnp.bfloat16)
    return (projected, rotated_basis.reshape(NBLK, COARSE, NVEC), rotated_images.reshape(NBLK, COARSE, NVEC))
```

```python
import functools
import math

import jax
import jax.numpy as jnp
from jax import lax
from jax.experimental import pallas as pl
from jax.experimental.pallas import tpu as pltpu
from jax.sharding import PartitionSpec as P

MESH = pl.DeviceIdType.MESH
F32, BF16 = jnp.float32, jnp.bfloat16
PLANE = [(dx, dy) for dx in range(4) for dy in range(4) if dx or dy]
PLANE.sort(key=lambda d: -(min(d[0], 4 - d[0]) + min(d[1], 4 - d[1])))
DEPTH = (4, 3, 5, 2, 6, 1, 7)


def dot(a, b, ca, cb):
    return lax.dot_general(a, b, (((ca,), (cb,)), ((), ())), preferred_element_type=F32)


def iota(shape, dim):
    return lax.broadcasted_iota(jnp.int32, shape, dim)


def kernel(
    scale, basis, images, hops, neighbours, rotation, proj_out, basis_out, images_out,
    a_v, i_v, h_v, r_v, nb_s, piece, wide, gath, part, core_in, half, plane_out, plane_in, depth_buf, gathered,
    rot_part, new_part, new_core, new_plane, new_depth, new_full,
    load_sem, hop_load, halo_send, halo_recv, forward_send, forward_recv, core_sem, plane_send, plane_recv,
    depth_send, depth_recv, gather_send, gather_recv, pass_send, pass_recv,
    ncore_sem, nplane_send, nplane_recv, ndepth_send, ndepth_recv, nlast_sem,
):
    site, mode = lax.axis_index("site"), lax.axis_index("mode")
    y, z, x_lo = site % 4, (site // 4) % 8, site // 32
    core, x_hi = mode % 2, mode // 2
    x = x_hi * 2 + x_lo
    slot = x * 4 + y
    t, r = site // 8, site % 8

    def device(px, py, pz, pc):
        return ((px % 2) * 32 + pz * 4 + py, (px // 2) * 2 + pc)

    other = (site, x_hi * 2 + 1 - core)
    far = (mode + 2) % 4
    mate, far_mate = other[1], (other[1] + 2) % 4
    plane = [((x + dx) % 4, (y + dy) % 4) for dx, dy in PLANE]
    deep = [(z + d) % 8 for d in DEPTH]
    sites = {
        1: t * 8 + (r + 4) % 8,
        2: t * 8 + r // 4 * 4 + (r % 4 + 2) % 4,
        3: t * 8 + r // 2 * 2 + (r + 1) % 2,
        4: ((t + 7) % 8) * 8 + r,
        5: ((t + 1) % 8) * 8 + r,
    }

    loads = [
        pltpu.make_async_copy(src, dst, load_sem.at[n])
        for n, (src, dst) in enumerate(((basis, a_v), (images, i_v), (rotation, r_v), (neighbours, nb_s)))
    ]
    for copy in loads:
        copy.start()
    hop_loads = [pltpu.make_async_copy(hops.at[h], h_v.at[h], hop_load.at[h]) for h in range(9)]
    for copy in hop_loads:
        copy.start()

    barrier = pltpu.get_barrier_semaphore()
    greeted = [other] + [device(px, py, z, core) for px, py in plane] + [device(x, y, pz, core) for pz in deep]
    greeted += [(sites[1], far)] + [(sites[k], m) for k in (4, 5) for m in (mode, far)]
    for peer in greeted:
        pl.semaphore_signal(barrier, inc=1, device_id=peer, device_id_type=MESH)

    def remote(src, dst, send_sem, recv_sem, peer):
        copy = pltpu.make_async_remote_copy(
            src_ref=src, dst_ref=dst, send_sem=send_sem, recv_sem=recv_sem, device_id=peer, device_id_type=MESH
        )
        return copy

    def arrived(dst, send_sem, recv_sem):
        remote(dst, dst, send_sem, recv_sem, other).wait_recv()

    loads[0].wait()
    spread = (
        (iota((128, 128), 0) - 112 == iota((128, 128), 1) % 16) & (iota((128, 128), 0) >= 112)
    ).astype(F32).astype(BF16)
    own_lanes = iota((800, 128), 0) % 8 == iota((800, 128), 1) // 16
    repeated = dot(a_v[:, 384:512], spread, 1, 0)
    repeated = jnp.where(own_lanes, repeated, 0.0).astype(BF16)
    put = (iota((800, 128), 0) // 8 + 100 * mode) % 128 == iota((800, 128), 1)
    piece[0, mode] = dot(repeated, put.astype(F32).astype(BF16), 0, 0).astype(BF16)

    loads[1].wait()
    part[:, 0:384] = dot(a_v[...], i_v[:, 0:384], 0, 0)
    part[:, 384:496] = dot(a_v[...], i_v[:, 384:496], 0, 0)
    part[:, 496:512] = jnp.zeros((512, 16), F32)

    pl.semaphore_wait(barrier, len(greeted))

    sent = []

    def start(copy):
        copy.start()
        sent.append(copy)

    mine = piece.at[0, mode]
    for k, m in ((4, far), (5, far), (4, mode), (5, mode), (2, far), (1, far), (3, far), (0, far), (2, mode), (1, mode), (3, mode)):
        target = site if k == 0 else sites[k]
        start(remote(mine, piece.at[k, mode], halo_send.at[k, m // 2], halo_recv.at[k, mode // 2], (target, m)))
    start(remote(mine, piece.at[0, mode], forward_send.at[0, x_hi], forward_recv.at[0, x_hi], other))
    start(
        remote(
            part.at[pl.ds(256 * (1 - core), 256)], core_in, core_sem.at[0], core_sem.at[1], other
        )
    )

    loads[2].wait()
    basis_out[...] = dot(a_v[...], r_v[...], 1, 0).astype(BF16)

    arrived(core_in, core_sem.at[0], core_sem.at[1])
    summed = part[pl.ds(256 * core, 256), :] + core_in[...]
    for j in range(16):
        half[j] = summed[16 * j : 16 * j + 16]
    plane_out[...] = half[...].astype(BF16)
    for n, (px, py) in enumerate(plane):
        start(remote(plane_out.at[4 * px + py], plane_in.at[n], plane_send.at[n], plane_recv.at[n], device(px, py, z, core)))

    rot_part[...] = dot(i_v[...], r_v[0:496, :], 1, 0)

    for k, m in ((3, mode), (1, mode), (0, far), (2, mode), (3, far), (1, far), (2, far), (4, mode), (5, mode), (4, far), (5, far)):
        arrived(piece.at[k, m], halo_send.at[k, m // 2], halo_recv.at[k, m // 2])
        start(remote(piece.at[k, m], piece.at[k, m], forward_send.at[k, m // 2], forward_recv.at[k, m // 2], other))

    lane = iota((8, 16, 128), 2)
    for k in range(6):
        for m in (mate, far_mate):
            arrived(piece.at[k, m], forward_send.at[k, m // 2], forward_recv.at[k, m // 2])
        p0, p1, p2, p3 = (piece[k, m] for m in range(4))
        rows = pl.ds(8 * k, 8)
        p0, p1, p2, p3 = (p.reshape(8, 16, 128) for p in (p0, p1, p2, p3))
        wide[rows, :, 0:128] = jnp.where(lane < 100, p0, p1)
        wide[rows, :, 128:256] = jnp.where(lane < 72, p1, p2)
        wide[rows, :, 256:384] = jnp.where(lane < 44, p2, p3)
        wide[rows, :, 384:512] = p3

    for n in range(15):
        arrived(plane_in.at[n], plane_send.at[n], plane_recv.at[n])
    total = half[slot]
    for n in range(15):
        total = total + plane_in[n].astype(F32)
    depth_buf[z] = total
    for n, pz in enumerate(deep):
        start(remote(depth_buf.at[z], depth_buf.at[z], depth_send.at[n], depth_recv.at[z], device(x, y, pz, core)))

    loads[3].wait()
    for h in range(9):
        for b in range(8):
            e = b if h == 0 else nb_s[b, h - 1]
            gath[h, 16 * b : 16 * b + 16, :] = wide[e]
    image = None
    for h in range(9):
        hop_loads[h].wait()
        term = dot(h_v[h], gath[h, :, 0:400], 1, 1)
        image = term if image is None else image + term
    image = jnp.where(own_lanes, image, 0.0).astype(BF16)

    by_block = dot(image, a_v[...], 0, 0)
    new = by_block[0:16]
    for b in range(1, 8):
        new = new + by_block[16 * b : 16 * b + 16]
    new_part[0] = new[:, 0:256]
    new_part[1] = new[:, 256:512]
    start(remote(new_part.at[1 - core], new_core, ncore_sem.at[0], ncore_sem.at[1], other))

    last = jnp.concatenate([r_v[496:512, :]] * 8, axis=0)
    images_out[...] = (rot_part[...] + dot(image, last, 1, 0)).astype(BF16)

    arrived(new_core, ncore_sem.at[0], ncore_sem.at[1])
    new_plane[slot] = (new_part[core] + new_core[...]).astype(BF16)
    for n, (px, py) in enumerate(plane):
        start(remote(new_plane.at[slot], new_plane.at[slot], nplane_send.at[n], nplane_recv.at[slot], device(px, py, z, core)))

    for pz in deep:
        arrived(depth_buf.at[pz], depth_send.at[0], depth_recv.at[pz])
    total = depth_buf[0]
    for n in range(1, 8):
        total = total + depth_buf[n]
    gathered[16 * core + slot] = (total * scale).astype(BF16)
    own = gathered.at[16 * core + slot]
    for n, (px, py) in enumerate(plane):
        start(remote(own, own, gather_send.at[n], gather_recv.at[slot], device(px, py, z, core)))
    start(remote(own, own, pass_send.at[slot], pass_recv.at[slot], other))

    for px, py in plane:
        q = 4 * px + py
        arrived(new_plane.at[q], nplane_send.at[0], nplane_recv.at[q])
    total = new_plane[0].astype(F32)
    for n in range(1, 16):
        total = total + new_plane[n].astype(F32)
    new_depth[z] = total
    for n, pz in enumerate(deep):
        start(remote(new_depth.at[z], new_depth.at[z], ndepth_send.at[n], ndepth_recv.at[z], device(x, y, pz, core)))

    for px, py in plane[::-1]:
        q = 4 * px + py
        block = gathered.at[16 * core + q]
        arrived(block, gather_send.at[0], gather_recv.at[q])
        start(remote(block, block, pass_send.at[q], pass_recv.at[q], other))
    for q in range(16):
        arrived(gathered.at[16 * (1 - core) + q], pass_send.at[0], pass_recv.at[q])
    for q in range(32):
        proj_out[16 * q : 16 * q + 16, :] = gathered[q].astype(F32)

    for pz in deep:
        arrived(new_depth.at[pz], ndepth_send.at[0], ndepth_recv.at[pz])
    total = new_depth[0]
    for n in range(1, 8):
        total = total + new_depth[n]
    new_full[core] = total * scale
    start(remote(new_full.at[core], new_full.at[core], nlast_sem.at[0], nlast_sem.at[1], other))
    arrived(new_full.at[1 - core], nlast_sem.at[0], nlast_sem.at[1])
    for n in range(2):
        proj_out[256 * n : 256 * n + 256, 496:512] = new_full[n].T

    for copy in sent:
        copy.wait_send()


def local(basis, images, hops, neighbours, rotation):
    blocks, modes, nvec = basis.shape
    old = images.shape[2]
    rows = blocks * modes
    sites = lax.axis_size("site") * lax.axis_size("mode")
    scale = 1.0 / math.sqrt(rows * sites)
    flat = lambda v: jnp.transpose(v, (1, 0, 2)).reshape(rows, v.shape[2])
    by_hop = jnp.transpose(hops, (1, 2, 0, 3)).reshape(9, rows, hops.shape[3])
    anywhere = pl.BlockSpec(memory_space=pl.ANY)
    vmem = pl.BlockSpec(memory_space=pltpu.VMEM)
    dma = pltpu.SemaphoreType.DMA
    projected, rotated_basis, rotated_images = pl.pallas_call(
        functools.partial(kernel, scale),
        out_shape=(
            jax.ShapeDtypeStruct((nvec, nvec), F32),
            jax.ShapeDtypeStruct((rows, nvec), BF16),
            jax.ShapeDtypeStruct((rows, nvec), BF16),
        ),
        in_specs=[anywhere] * 5,
        out_specs=(vmem, vmem, vmem),
        scratch_shapes=[
            pltpu.VMEM((rows, nvec), BF16),
            pltpu.VMEM((rows, old), BF16),
            pltpu.VMEM(by_hop.shape, BF16),
            pltpu.VMEM((nvec, nvec), BF16),
            pltpu.SMEM((8, 8), jnp.int32),
            pltpu.VMEM((6, 4, 128, 128), BF16),
            pltpu.VMEM((48, 16, 512), BF16),
            pltpu.VMEM((9, 128, 512), BF16),
            pltpu.VMEM((512, 512), F32),
            pltpu.VMEM((256, 512), F32),
            pltpu.VMEM((16, 16, 512), F32),
            pltpu.VMEM((16, 16, 512), BF16),
            pltpu.VMEM((15, 16, 512), BF16),
            pltpu.VMEM((8, 16, 512), F32),
            pltpu.VMEM((32, 16, 512), BF16),
            pltpu.VMEM((rows, nvec), F32),
            pltpu.VMEM((2, 16, 256), F32),
            pltpu.VMEM((16, 256), F32),
            pltpu.VMEM((16, 16, 256), BF16),
            pltpu.VMEM((8, 16, 256), F32),
            pltpu.VMEM((2, 16, 256), F32),
            dma((4,)),
            dma((9,)),
            dma((6, 2)),
            dma((6, 2)),
            dma((6, 2)),
            dma((6, 2)),
            dma((2,)),
            dma((15,)),
            dma((15,)),
            dma((7,)),
            dma((8,)),
            dma((15,)),
            dma((16,)),
            dma((16,)),
            dma((16,)),
            dma((2,)),
            dma((15,)),
            dma((16,)),
            dma((7,)),
            dma((8,)),
            dma((2,)),
        ],
        compiler_params=pltpu.CompilerParams(
            collective_id=0, has_side_effects=True, vmem_limit_bytes=60 * 2**20
        ),
    )(flat(basis), flat(images), by_hop, neighbours, rotation)
    unflat = lambda v: jnp.transpose(v.reshape(modes, blocks, nvec), (1, 0, 2))
    return projected, unflat(rotated_basis), unflat(rotated_images)


def solution(mesh):
    placed = (
        P("site", "mode", None),
        P("site", "mode", None),
        P("site", None, "mode", None),
        P("site", None),
        P(),
    )
    return jax.shard_map(
        local,
        mesh=mesh,
        in_specs=placed,
        out_specs=(P(), P("site", "mode", None), P("site", "mode", None)),
        check_vma=False,
    )
```

```python
import functools
import math

import jax
import jax.numpy as jnp
from jax import lax
from jax.experimental import pallas as pl
from jax.experimental.pallas import tpu as pltpu
from jax.sharding import PartitionSpec as P

MESH = pl.DeviceIdType.MESH
F32, BF16 = jnp.float32, jnp.bfloat16
PLANE = [(dx, dy) for dx in range(4) for dy in range(4) if dx or dy]
PLANE.sort(key=lambda d: -(min(d[0], 4 - d[0]) + min(d[1], 4 - d[1])))
DEPTH = (4, 3, 5, 2, 6, 1, 7)


def dot(a, b, ca, cb):
    return lax.dot_general(a, b, (((ca,), (cb,)), ((), ())), preferred_element_type=F32)


def iota(shape, dim):
    return lax.broadcasted_iota(jnp.int32, shape, dim)


def kernel(
    scale, basis, images, hops, neighbours, rotation, proj_out, basis_out, images_out,
    a_v, i_v, h_v, r_v, nb_s, piece, wide, gath, part, image_sum, core_in, half, plane_out, plane_in, depth_buf, gathered,
    rot_part, new_part, new_core, new_plane, new_depth,
    load_sem, hop_load, halo_send, halo_recv, forward_send, forward_recv, core_sem, plane_send, plane_recv,
    depth_send, depth_recv, gather_send, gather_recv, pass_send, pass_recv,
    ncore_sem, nplane_send, nplane_recv, ndepth_send, ndepth_recv,
):
    site, mode = lax.axis_index("site"), lax.axis_index("mode")
    y, z, x_lo = site % 4, (site // 4) % 8, site // 32
    core, x_hi = mode % 2, mode // 2
    x = x_hi * 2 + x_lo
    slot = x * 4 + y
    t, r = site // 8, site % 8

    def device(px, py, pz, pc):
        return ((px % 2) * 32 + pz * 4 + py, (px // 2) * 2 + pc)

    other = (site, x_hi * 2 + 1 - core)
    far = (mode + 2) % 4
    mate, far_mate = other[1], (other[1] + 2) % 4
    plane = [((x + dx) % 4, (y + dy) % 4) for dx, dy in PLANE]
    deep = [(z + d) % 8 for d in DEPTH]
    sites = {
        1: t * 8 + (r + 4) % 8,
        2: t * 8 + r // 4 * 4 + (r % 4 + 2) % 4,
        3: t * 8 + r // 2 * 2 + (r + 1) % 2,
        4: ((t + 7) % 8) * 8 + r,
        5: ((t + 1) % 8) * 8 + r,
    }

    barrier = pltpu.get_barrier_semaphore()
    greeted = [other] + [device(px, py, z, core) for px, py in plane] + [device(x, y, pz, c) for pz in deep for c in (core, 1 - core)]
    greeted += [(sites[1], far)] + [(sites[k], m) for k in (4, 5) for m in (mode, far)]
    for peer in greeted:
        pl.semaphore_signal(barrier, inc=1, device_id=peer, device_id_type=MESH)

    loads = [
        pltpu.make_async_copy(src, dst, load_sem.at[n])
        for n, (src, dst) in enumerate(((basis, a_v), (images, i_v), (rotation, r_v), (neighbours, nb_s)))
    ]
    for copy in loads:
        copy.start()
    hop_loads = [pltpu.make_async_copy(hops.at[h], h_v.at[h], hop_load.at[h]) for h in range(9)]
    for copy in hop_loads:
        copy.start()

    def remote(src, dst, send_sem, recv_sem, peer):
        copy = pltpu.make_async_remote_copy(
            src_ref=src, dst_ref=dst, send_sem=send_sem, recv_sem=recv_sem, device_id=peer, device_id_type=MESH
        )
        return copy

    def arrived(dst, send_sem, recv_sem):
        remote(dst, dst, send_sem, recv_sem, other).wait_recv()

    loads[0].wait()
    spread = (
        (iota((128, 128), 0) - 112 == iota((128, 128), 1) % 16) & (iota((128, 128), 0) >= 112)
    ).astype(F32).astype(BF16)
    own_lanes = iota((800, 128), 0) % 8 == iota((800, 128), 1) // 16
    repeated = dot(a_v[:, 384:512], spread, 1, 0)
    repeated = jnp.where(own_lanes, repeated, 0.0).astype(BF16)
    put = (iota((800, 128), 0) // 8 + 100 * mode) % 128 == iota((800, 128), 1)
    piece[0, mode] = dot(repeated, put.astype(F32).astype(BF16), 0, 0).astype(BF16)

    loads[1].wait()
    part[:, 0:384] = dot(a_v[...], i_v[:, 0:384], 0, 0)
    part[:, 384:496] = dot(a_v[...], i_v[:, 384:496], 0, 0)
    part[:, 496:512] = jnp.zeros((512, 16), F32)

    pl.semaphore_wait(barrier, len(greeted))

    sent = []

    def start(copy):
        copy.start()
        sent.append(copy)

    mine = piece.at[0, mode]
    for k, m in ((4, far), (5, far), (4, mode), (5, mode), (2, far), (1, far), (3, far), (0, far), (2, mode), (1, mode), (3, mode)):
        target = site if k == 0 else sites[k]
        start(remote(mine, piece.at[k, mode], halo_send.at[k, m // 2], halo_recv.at[k, mode // 2], (target, m)))
    start(remote(mine, piece.at[0, mode], forward_send.at[0, x_hi], forward_recv.at[0, x_hi], other))
    start(
        remote(
            part.at[pl.ds(256 * (1 - core), 256)], core_in, core_sem.at[0], core_sem.at[1], other
        )
    )

    loads[2].wait()
    basis_out[...] = dot(a_v[...], r_v[...], 1, 0).astype(BF16)

    arrived(core_in, core_sem.at[0], core_sem.at[1])
    summed = part[pl.ds(256 * core, 256), :] + core_in[...]
    for j in range(16):
        half[j] = summed[16 * j : 16 * j + 16]
    plane_out[...] = half[...].astype(BF16)
    for n, (px, py) in enumerate(plane):
        start(remote(plane_out.at[4 * px + py], plane_in.at[n], plane_send.at[n], plane_recv.at[n], device(px, py, z, core)))

    rot_part[...] = dot(i_v[...], r_v[0:496, :], 1, 0)

    lane = iota((8, 16, 128), 2)

    def forward(where):
        for k, m in where:
            arrived(piece.at[k, m], halo_send.at[k, m // 2], halo_recv.at[k, m // 2])
            start(remote(piece.at[k, m], piece.at[k, m], forward_send.at[k, m // 2], forward_recv.at[k, m // 2], other))

    def widen(groups):
        for k in groups:
            for m in (mate, far_mate):
                arrived(piece.at[k, m], forward_send.at[k, m // 2], forward_recv.at[k, m // 2])
            p0, p1, p2, p3 = (piece[k, m].reshape(8, 16, 128) for m in range(4))
            rows = pl.ds(8 * k, 8)
            wide[rows, :, 0:128] = jnp.where(lane < 100, p0, p1)
            wide[rows, :, 128:256] = jnp.where(lane < 72, p1, p2)
            wide[rows, :, 256:384] = jnp.where(lane < 44, p2, p3)
            wide[rows, :, 384:512] = p3

    def gather_rows(h):
        for b in range(8):
            e = b if h == 0 else nb_s[b, h - 1]
            gath[h, 16 * b : 16 * b + 16, :] = wide[e]

    def stencil(hs):
        for h in hs:
            gather_rows(h)
            hop_loads[h].wait()
        for c in range(5):
            rows = pl.ds(160 * c, 160)
            term = None if hs[0] == 0 else image_sum[rows, :]
            for h in hs:
                product = dot(h_v[h, rows, :], gath[h, :, 0:400], 1, 1)
                term = product if term is None else term + product
            image_sum[rows, :] = term

    forward(((3, mode), (1, mode), (0, far), (2, mode), (3, far), (1, far), (2, far)))
    widen((0, 1, 2, 3))
    loads[3].wait()
    stencil((0, 1, 2, 3))
    forward(((4, mode), (5, mode), (4, far), (5, far)))
    stencil((4, 5, 6))

    for n in range(15):
        arrived(plane_in.at[n], plane_send.at[n], plane_recv.at[n])
    total = half[slot]
    for n in range(15):
        total = total + plane_in[n].astype(F32)
    depth_buf[z] = total
    for n, pz in enumerate(deep):
        start(remote(depth_buf.at[z], depth_buf.at[z], depth_send.at[n], depth_recv.at[z], device(x, y, pz, core)))

    widen((4, 5))
    stencil((7, 8))
    image = jnp.where(own_lanes, image_sum[...], 0.0).astype(BF16)

    by_block = dot(image, a_v[...], 0, 0)
    new = by_block[0:16]
    for b in range(1, 8):
        new = new + by_block[16 * b : 16 * b + 16]
    new_part[0] = new[:, 0:256]
    new_part[1] = new[:, 256:512]
    start(remote(new_part.at[1 - core], new_core, ncore_sem.at[0], ncore_sem.at[1], other))

    last = jnp.concatenate([r_v[496:512, :]] * 8, axis=0)
    images_out[...] = (rot_part[...] + dot(image, last, 1, 0)).astype(BF16)

    arrived(new_core, ncore_sem.at[0], ncore_sem.at[1])
    new_plane[slot] = (new_part[core] + new_core[...]).astype(BF16)
    for n, (px, py) in enumerate(plane):
        start(remote(new_plane.at[slot], new_plane.at[slot], nplane_send.at[n], nplane_recv.at[slot], device(px, py, z, core)))

    for pz in deep:
        arrived(depth_buf.at[pz], depth_send.at[0], depth_recv.at[pz])
    total = depth_buf[0]
    for n in range(1, 8):
        total = total + depth_buf[n]
    gathered[16 * core + slot] = (total * scale).astype(BF16)
    own = gathered.at[16 * core + slot]
    for n, (px, py) in enumerate(plane):
        start(remote(own, own, gather_send.at[n], gather_recv.at[slot], device(px, py, z, core)))
    start(remote(own, own, pass_send.at[slot], pass_recv.at[slot], other))

    for px, py in plane:
        q = 4 * px + py
        arrived(new_plane.at[q], nplane_send.at[0], nplane_recv.at[q])
    total = new_plane[0].astype(F32)
    for n in range(1, 16):
        total = total + new_plane[n].astype(F32)
    new_depth[core, z] = total.astype(BF16)
    own = new_depth.at[core, z]
    for n, pz in enumerate(deep):
        for c in (core, 1 - core):
            start(remote(own, own, ndepth_send.at[n, c], ndepth_recv.at[core, z], device(x, y, pz, c)))
    start(remote(own, own, ndepth_send.at[7, 0], ndepth_recv.at[core, z], other))

    def put_out(q):
        proj_out[pl.ds(pl.multiple_of(16 * q, 16), 16), :] = gathered[q].astype(F32)

    put_out(16 * core + slot)
    for px, py in plane[::-1]:
        q = 4 * px + py
        block = gathered.at[16 * core + q]
        arrived(block, gather_send.at[0], gather_recv.at[q])
        start(remote(block, block, pass_send.at[q], pass_recv.at[q], other))
        put_out(16 * core + q)
    for q in range(16):
        arrived(gathered.at[16 * (1 - core) + q], pass_send.at[0], pass_recv.at[q])
        put_out(16 * (1 - core) + q)

    for pz in deep:
        arrived(new_depth.at[core, pz], ndepth_send.at[0, 0], ndepth_recv.at[core, pz])
    for pz in [z] + deep:
        arrived(new_depth.at[1 - core, pz], ndepth_send.at[0, 0], ndepth_recv.at[1 - core, pz])
    for c in range(2):
        total = new_depth[c, 0].astype(F32)
        for n in range(1, 8):
            total = total + new_depth[c, n].astype(F32)
        proj_out[256 * c : 256 * c + 256, 496:512] = (total * scale).T

    for copy in sent:
        copy.wait_send()


def finish(*refs):
    copies = [pltpu.make_async_copy(refs[n], refs[3 + n], refs[6].at[n]) for n in range(3)]
    for copy in copies:
        copy.start()
    for copy in copies:
        copy.wait()


def local(basis, images, hops, neighbours, rotation):
    blocks, modes, nvec = basis.shape
    old = images.shape[2]
    rows = blocks * modes
    sites = lax.axis_size("site") * lax.axis_size("mode")
    scale = 1.0 / math.sqrt(rows * sites)
    flat = lambda v: jnp.transpose(v, (1, 0, 2)).reshape(rows, v.shape[2])
    by_hop = jnp.transpose(hops, (1, 2, 0, 3)).reshape(9, rows, hops.shape[3])
    hbm = pl.BlockSpec(memory_space=pltpu.HBM)
    vmem = pl.BlockSpec(memory_space=pltpu.VMEM)
    dma = pltpu.SemaphoreType.DMA
    projected, rotated_basis, rotated_images = pl.pallas_call(
        functools.partial(kernel, scale),
        out_shape=(
            pltpu.VMEM((nvec, nvec), F32),
            pltpu.VMEM((rows, nvec), BF16),
            pltpu.VMEM((rows, nvec), BF16),
        ),
        in_specs=[hbm] * 5,
        out_specs=(vmem, vmem, vmem),
        scratch_shapes=[
            pltpu.VMEM((rows, nvec), BF16),
            pltpu.VMEM((rows, old), BF16),
            pltpu.VMEM(by_hop.shape, BF16),
            pltpu.VMEM((nvec, nvec), BF16),
            pltpu.SMEM((8, 8), jnp.int32),
            pltpu.VMEM((6, 4, 128, 128), BF16),
            pltpu.VMEM((48, 16, 512), BF16),
            pltpu.VMEM((9, 128, 512), BF16),
            pltpu.VMEM((512, 512), F32),
            pltpu.VMEM((rows, 128), F32),
            pltpu.VMEM((256, 512), F32),
            pltpu.VMEM((16, 16, 512), F32),
            pltpu.VMEM((16, 16, 512), BF16),
            pltpu.VMEM((15, 16, 512), BF16),
            pltpu.VMEM((8, 16, 512), F32),
            pltpu.VMEM((32, 16, 512), BF16),
            pltpu.VMEM((rows, nvec), F32),
            pltpu.VMEM((2, 16, 256), F32),
            pltpu.VMEM((16, 256), F32),
            pltpu.VMEM((16, 16, 256), BF16),
            pltpu.VMEM((2, 8, 16, 256), BF16),
            dma((4,)),
            dma((9,)),
            dma((6, 2)),
            dma((6, 2)),
            dma((6, 2)),
            dma((6, 2)),
            dma((2,)),
            dma((15,)),
            dma((15,)),
            dma((7,)),
            dma((8,)),
            dma((15,)),
            dma((16,)),
            dma((16,)),
            dma((16,)),
            dma((2,)),
            dma((15,)),
            dma((16,)),
            dma((8, 2)),
            dma((2, 8)),
        ],
        compiler_params=pltpu.CompilerParams(
            collective_id=0, has_side_effects=True, vmem_limit_bytes=40 * 2**20
        ),
    )(*(pltpu.with_memory_space_constraint(v, pltpu.HBM) for v in (flat(basis), flat(images), by_hop, neighbours, rotation)))
    projected, rotated_basis, rotated_images = pl.pallas_call(
        finish,
        out_shape=(
            jax.ShapeDtypeStruct((nvec, nvec), F32),
            jax.ShapeDtypeStruct((rows, nvec), BF16),
            jax.ShapeDtypeStruct((rows, nvec), BF16),
        ),
        in_specs=[pl.BlockSpec(memory_space=pl.ANY)] * 3,
        out_specs=(hbm, hbm, hbm),
        scratch_shapes=[dma((3,))],
        compiler_params=pltpu.CompilerParams(vmem_limit_bytes=2**20),
    )(projected, rotated_basis, rotated_images)
    unflat = lambda v: jnp.transpose(v.reshape(modes, blocks, nvec), (1, 0, 2))
    return projected, unflat(rotated_basis), unflat(rotated_images)


def solution(mesh):
    placed = (
        P("site", "mode", None),
        P("site", "mode", None),
        P("site", None, "mode", None),
        P("site", None),
        P(),
    )
    return jax.shard_map(
        local,
        mesh=mesh,
        in_specs=placed,
        out_specs=(P(), P("site", "mode", None), P("site", "mode", None)),
        check_vma=False,
    )
```

```python
import functools
import math

import jax
import jax.numpy as jnp
from jax import lax
from jax.experimental import pallas as pl
from jax.experimental.pallas import tpu as pltpu
from jax.sharding import PartitionSpec as P

MESH = pl.DeviceIdType.MESH
F32, BF16 = jnp.float32, jnp.bfloat16
PLANE = [(dx, dy) for dx in range(4) for dy in range(4) if dx or dy]
PLANE.sort(key=lambda d: -(min(d[0], 4 - d[0]) + min(d[1], 4 - d[1])))
AWAY = (2, 1, 3, 0)
DEPTH = (4, 3, 5, 2, 6, 1, 7)


def dot(a, b, ca, cb):
    return lax.dot_general(a, b, (((ca,), (cb,)), ((), ())), preferred_element_type=F32)


def iota(shape, dim):
    return lax.broadcasted_iota(jnp.int32, shape, dim)


def kernel(
    scale, basis, images, hops, neighbours, rotation, proj_out, basis_out, images_out,
    a_v, i_v, h_v, r_v, nb_s, piece, wide, gath, part, image_sum, core_in, half, plane_out, plane_in, depth_buf, gathered,
    rot_part, new_part, new_core, new_plane, new_depth,
    load_sem, hop_load, halo_send, halo_recv, forward_send, forward_recv, core_send, core_recv, plane_send, plane_recv,
    depth_send, depth_recv, gather_send, gather_recv, pass_send, pass_recv,
    ncore_sem, nplane_send, nplane_recv, ndepth_send, ndepth_recv,
):
    site, mode = lax.axis_index("site"), lax.axis_index("mode")
    y, z, x_lo = site % 4, (site // 4) % 8, site // 32
    core, x_hi = mode % 2, mode // 2
    x = x_hi * 2 + x_lo
    slot = x * 4 + y
    t, r = site // 8, site % 8

    def device(px, py, pz, pc):
        return ((px % 2) * 32 + pz * 4 + py, (px // 2) * 2 + pc)

    other = (site, x_hi * 2 + 1 - core)
    far = (mode + 2) % 4
    mate, far_mate = other[1], (other[1] + 2) % 4
    plane = [((x + dx) % 4, (y + dy) % 4) for dx, dy in PLANE]
    deep = [(z + d) % 8 for d in DEPTH]
    sites = {
        1: t * 8 + (r + 4) % 8,
        2: t * 8 + r // 4 * 4 + (r % 4 + 2) % 4,
        3: t * 8 + r // 2 * 2 + (r + 1) % 2,
        4: ((t + 7) % 8) * 8 + r,
        5: ((t + 1) % 8) * 8 + r,
    }

    barrier = pltpu.get_barrier_semaphore()
    greeted = [other] + [device(px, py, z, core) for px, py in plane] + [device(x, y, pz, c) for pz in deep for c in (core, 1 - core)]
    greeted += [(sites[1], far)] + [(sites[k], m) for k in (4, 5) for m in (mode, far)]
    for peer in greeted:
        pl.semaphore_signal(barrier, inc=1, device_id=peer, device_id_type=MESH)

    loads = [
        pltpu.make_async_copy(src, dst, load_sem.at[n])
        for n, (src, dst) in enumerate(((basis, a_v), (images, i_v), (rotation, r_v), (neighbours, nb_s)))
    ]
    for copy in loads:
        copy.start()

    def remote(src, dst, send_sem, recv_sem, peer):
        copy = pltpu.make_async_remote_copy(
            src_ref=src, dst_ref=dst, send_sem=send_sem, recv_sem=recv_sem, device_id=peer, device_id_type=MESH
        )
        return copy

    def arrived(dst, send_sem, recv_sem):
        remote(dst, dst, send_sem, recv_sem, other).wait_recv()

    loads[0].wait()
    spread = (
        (iota((128, 128), 0) - 112 == iota((128, 128), 1) % 16) & (iota((128, 128), 0) >= 112)
    ).astype(F32).astype(BF16)
    own_lanes = iota((800, 128), 0) % 8 == iota((800, 128), 1) // 16
    repeated = dot(a_v[:, 384:512], spread, 1, 0)
    repeated = jnp.where(own_lanes, repeated, 0.0).astype(BF16)
    put = (iota((800, 128), 0) // 8 + 100 * mode) % 128 == iota((800, 128), 1)
    piece[0, mode] = dot(repeated, put.astype(F32).astype(BF16), 0, 0).astype(BF16)

    loads[1].wait()
    hop_loads = [pltpu.make_async_copy(hops.at[h], h_v.at[h], hop_load.at[h]) for h in range(9)]
    for copy in hop_loads:
        copy.start()
    part[:, 0:384] = dot(a_v[...], i_v[:, 0:384], 0, 0)
    part[:, 384:496] = dot(a_v[...], i_v[:, 384:496], 0, 0)
    part[:, 496:512] = jnp.zeros((512, 16), F32)

    pl.semaphore_wait(barrier, len(greeted))

    sent = []

    def start(copy):
        copy.start()
        sent.append(copy)

    mine = piece.at[0, mode]
    for k, m in ((4, far), (5, far), (4, mode), (5, mode), (2, far), (1, far), (3, far), (0, far), (2, mode), (1, mode), (3, mode)):
        target = site if k == 0 else sites[k]
        start(remote(mine, piece.at[k, mode], halo_send.at[k, m // 2], halo_recv.at[k, mode // 2], (target, m)))
    start(remote(mine, piece.at[0, mode], forward_send.at[0, x_hi], forward_recv.at[0, x_hi], other))
    columns = [(x + dx) % 4 for dx in AWAY]

    def quarter(c, px):
        return pl.ds(pl.multiple_of(256 * c + 64 * px, 64), 64)

    for n, px in enumerate(columns):
        start(remote(part.at[quarter(1 - core, px)], core_in.at[px], core_send.at[n], core_recv.at[n], other))

    loads[2].wait()
    basis_out[...] = dot(a_v[...], r_v[...], 1, 0).astype(BF16)

    for n, px in enumerate(columns):
        arrived(core_in.at[px], core_send.at[n], core_recv.at[n])
        summed = part[quarter(core, px), :] + core_in[px]
        for q in range(4):
            half[4 * px + q] = summed[16 * q : 16 * q + 16]
            plane_out[4 * px + q] = summed[16 * q : 16 * q + 16].astype(BF16)
        for dy in AWAY:
            if AWAY[n] or dy:
                py, k = (y + dy) % 4, PLANE.index((AWAY[n], dy))
                start(remote(plane_out.at[4 * px + py], plane_in.at[k], plane_send.at[k], plane_recv.at[k], device(px, py, z, core)))

    rot_part[...] = dot(i_v[...], r_v[0:496, :], 1, 0)

    lane = iota((8, 16, 128), 2)

    def forward(where):
        for k, m in where:
            arrived(piece.at[k, m], halo_send.at[k, m // 2], halo_recv.at[k, m // 2])
            start(remote(piece.at[k, m], piece.at[k, m], forward_send.at[k, m // 2], forward_recv.at[k, m // 2], other))

    def widen(groups):
        for k in groups:
            for m in (mate, far_mate):
                arrived(piece.at[k, m], forward_send.at[k, m // 2], forward_recv.at[k, m // 2])
            p0, p1, p2, p3 = (piece[k, m].reshape(8, 16, 128) for m in range(4))
            rows = pl.ds(8 * k, 8)
            wide[rows, :, 0:128] = jnp.where(lane < 100, p0, p1)
            wide[rows, :, 128:256] = jnp.where(lane < 72, p1, p2)
            wide[rows, :, 256:384] = jnp.where(lane < 44, p2, p3)
            wide[rows, :, 384:512] = p3

    def gather_rows(h):
        for b in range(8):
            e = b if h == 0 else nb_s[b, h - 1]
            gath[h, 16 * b : 16 * b + 16, :] = wide[e]

    def stencil(hs):
        for h in hs:
            gather_rows(h)
            hop_loads[h].wait()
        for c in range(5):
            rows = pl.ds(160 * c, 160)
            term = None if hs[0] == 0 else image_sum[rows, :]
            for h in hs:
                product = dot(h_v[h, rows, :], gath[h, :, 0:400], 1, 1)
                term = product if term is None else term + product
            image_sum[rows, :] = term

    forward(((3, mode), (1, mode), (0, far), (2, mode), (3, far), (1, far), (2, far)))
    widen((0, 1, 2, 3))
    loads[3].wait()
    for n in range(15):
        arrived(plane_in.at[n], plane_send.at[n], plane_recv.at[n])
    total = half[slot]
    for n in range(15):
        total = total + plane_in[n].astype(F32)
    depth_buf[z] = total
    for n, pz in enumerate(deep):
        start(remote(depth_buf.at[z], depth_buf.at[z], depth_send.at[n], depth_recv.at[z], device(x, y, pz, core)))

    stencil((0, 1, 2, 3))
    forward(((4, mode), (5, mode), (4, far), (5, far)))
    stencil((4, 5, 6))

    widen((4, 5))
    stencil((7, 8))
    image = jnp.where(own_lanes, image_sum[...], 0.0).astype(BF16)

    by_block = dot(image, a_v[...], 0, 0)
    new = by_block[0:16]
    for b in range(1, 8):
        new = new + by_block[16 * b : 16 * b + 16]
    new_part[0] = new[:, 0:256]
    new_part[1] = new[:, 256:512]
    start(remote(new_part.at[1 - core], new_core, ncore_sem.at[0], ncore_sem.at[1], other))

    last = jnp.concatenate([r_v[496:512, :]] * 8, axis=0)
    images_out[...] = (rot_part[...] + dot(image, last, 1, 0)).astype(BF16)

    arrived(new_core, ncore_sem.at[0], ncore_sem.at[1])
    new_plane[slot] = (new_part[core] + new_core[...]).astype(BF16)
    for n, (px, py) in enumerate(plane):
        start(remote(new_plane.at[slot], new_plane.at[slot], nplane_send.at[n], nplane_recv.at[slot], device(px, py, z, core)))

    for pz in deep:
        arrived(depth_buf.at[pz], depth_send.at[0], depth_recv.at[pz])
    total = depth_buf[0]
    for n in range(1, 8):
        total = total + depth_buf[n]
    gathered[16 * core + slot] = (total * scale).astype(BF16)
    own = gathered.at[16 * core + slot]
    for n, (px, py) in enumerate(plane):
        start(remote(own, own, gather_send.at[n], gather_recv.at[slot], device(px, py, z, core)))
    start(remote(own, own, pass_send.at[slot], pass_recv.at[slot], other))

    for px, py in plane:
        q = 4 * px + py
        arrived(new_plane.at[q], nplane_send.at[0], nplane_recv.at[q])
    total = new_plane[0].astype(F32)
    for n in range(1, 16):
        total = total + new_plane[n].astype(F32)
    new_depth[core, z] = total.astype(BF16)
    own = new_depth.at[core, z]
    for n, pz in enumerate(deep):
        for c in (core, 1 - core):
            start(remote(own, own, ndepth_send.at[n, c], ndepth_recv.at[core, z], device(x, y, pz, c)))
    start(remote(own, own, ndepth_send.at[7, 0], ndepth_recv.at[core, z], other))

    def put_out(q):
        proj_out[pl.ds(pl.multiple_of(16 * q, 16), 16), :] = gathered[q].astype(F32)

    put_out(16 * core + slot)
    for px, py in plane[::-1]:
        q = 4 * px + py
        block = gathered.at[16 * core + q]
        arrived(block, gather_send.at[0], gather_recv.at[q])
        start(remote(block, block, pass_send.at[q], pass_recv.at[q], other))
        put_out(16 * core + q)
    for q in range(16):
        arrived(gathered.at[16 * (1 - core) + q], pass_send.at[0], pass_recv.at[q])
        put_out(16 * (1 - core) + q)

    for pz in deep:
        arrived(new_depth.at[core, pz], ndepth_send.at[0, 0], ndepth_recv.at[core, pz])
    for pz in [z] + deep:
        arrived(new_depth.at[1 - core, pz], ndepth_send.at[0, 0], ndepth_recv.at[1 - core, pz])
    for c in range(2):
        total = new_depth[c, 0].astype(F32)
        for n in range(1, 8):
            total = total + new_depth[c, n].astype(F32)
        proj_out[256 * c : 256 * c + 256, 496:512] = (total * scale).T

    for copy in sent:
        copy.wait_send()


def finish(*refs):
    copies = [pltpu.make_async_copy(refs[n], refs[3 + n], refs[6].at[n]) for n in range(3)]
    for copy in copies:
        copy.start()
    for copy in copies:
        copy.wait()


def local(basis, images, hops, neighbours, rotation):
    blocks, modes, nvec = basis.shape
    old = images.shape[2]
    rows = blocks * modes
    sites = lax.axis_size("site") * lax.axis_size("mode")
    scale = 1.0 / math.sqrt(rows * sites)
    flat = lambda v: jnp.transpose(v, (1, 0, 2)).reshape(rows, v.shape[2])
    by_hop = jnp.transpose(hops, (1, 2, 0, 3)).reshape(9, rows, hops.shape[3])
    hbm = pl.BlockSpec(memory_space=pltpu.HBM)
    vmem = pl.BlockSpec(memory_space=pltpu.VMEM)
    dma = pltpu.SemaphoreType.DMA
    projected, rotated_basis, rotated_images = pl.pallas_call(
        functools.partial(kernel, scale),
        out_shape=(
            pltpu.VMEM((nvec, nvec), F32),
            pltpu.VMEM((rows, nvec), BF16),
            pltpu.VMEM((rows, nvec), BF16),
        ),
        in_specs=[hbm] * 5,
        out_specs=(vmem, vmem, vmem),
        scratch_shapes=[
            pltpu.VMEM((rows, nvec), BF16),
            pltpu.VMEM((rows, old), BF16),
            pltpu.VMEM(by_hop.shape, BF16),
            pltpu.VMEM((nvec, nvec), BF16),
            pltpu.SMEM((8, 8), jnp.int32),
            pltpu.VMEM((6, 4, 128, 128), BF16),
            pltpu.VMEM((48, 16, 512), BF16),
            pltpu.VMEM((9, 128, 512), BF16),
            pltpu.VMEM((512, 512), F32),
            pltpu.VMEM((rows, 128), F32),
            pltpu.VMEM((4, 64, 512), F32),
            pltpu.VMEM((16, 16, 512), F32),
            pltpu.VMEM((16, 16, 512), BF16),
            pltpu.VMEM((15, 16, 512), BF16),
            pltpu.VMEM((8, 16, 512), F32),
            pltpu.VMEM((32, 16, 512), BF16),
            pltpu.VMEM((rows, nvec), F32),
            pltpu.VMEM((2, 16, 256), F32),
            pltpu.VMEM((16, 256), F32),
            pltpu.VMEM((16, 16, 256), BF16),
            pltpu.VMEM((2, 8, 16, 256), BF16),
            dma((4,)),
            dma((9,)),
            dma((6, 2)),
            dma((6, 2)),
            dma((6, 2)),
            dma((6, 2)),
            dma((4,)),
            dma((4,)),
            dma((15,)),
            dma((15,)),
            dma((7,)),
            dma((8,)),
            dma((15,)),
            dma((16,)),
            dma((16,)),
            dma((16,)),
            dma((2,)),
            dma((15,)),
            dma((16,)),
            dma((8, 2)),
            dma((2, 8)),
        ],
        compiler_params=pltpu.CompilerParams(
            collective_id=0, has_side_effects=True, vmem_limit_bytes=40 * 2**20
        ),
    )(*(pltpu.with_memory_space_constraint(v, pltpu.HBM) for v in (flat(basis), flat(images), by_hop, neighbours, rotation)))
    projected, rotated_basis, rotated_images = pl.pallas_call(
        finish,
        out_shape=(
            jax.ShapeDtypeStruct((nvec, nvec), F32),
            jax.ShapeDtypeStruct((rows, nvec), BF16),
            jax.ShapeDtypeStruct((rows, nvec), BF16),
        ),
        in_specs=[pl.BlockSpec(memory_space=pl.ANY)] * 3,
        out_specs=(hbm, hbm, hbm),
        scratch_shapes=[dma((3,))],
        compiler_params=pltpu.CompilerParams(vmem_limit_bytes=2**20),
    )(projected, rotated_basis, rotated_images)
    unflat = lambda v: jnp.transpose(v.reshape(modes, blocks, nvec), (1, 0, 2))
    return projected, unflat(rotated_basis), unflat(rotated_images)


def solution(mesh):
    placed = (
        P("site", "mode", None),
        P("site", "mode", None),
        P("site", None, "mode", None),
        P("site", None),
        P(),
    )
    return jax.shard_map(
        local,
        mesh=mesh,
        in_specs=placed,
        out_specs=(P(), P("site", "mode", None), P("site", "mode", None)),
        check_vma=False,
    )
```

```python
import functools
import math

import jax
import jax.numpy as jnp
from jax import lax
from jax.experimental import pallas as pl
from jax.experimental.pallas import tpu as pltpu
from jax.sharding import PartitionSpec as P

MESH = pl.DeviceIdType.MESH
F32, BF16 = jnp.float32, jnp.bfloat16
PLANE = [(dx, dy) for dx in range(4) for dy in range(4) if dx or dy]
PLANE.sort(key=lambda d: -(min(d[0], 4 - d[0]) + min(d[1], 4 - d[1])))
AWAY = (2, 1, 3, 0)
DEPTH = (4, 3, 5, 2, 6, 1, 7)


def dot(a, b, ca, cb):
    return lax.dot_general(a, b, (((ca,), (cb,)), ((), ())), preferred_element_type=F32)


def iota(shape, dim):
    return lax.broadcasted_iota(jnp.int32, shape, dim)


def kernel(
    scale, basis, images, hops, neighbours, rotation, proj_out, basis_out, images_out,
    a_v, i_v, h_v, r_v, nb_s, piece, wide, gath, part, image_sum, core_in, half, plane_out, plane_in, depth_buf, gathered,
    rot_part, new_part, new_core, new_plane, new_depth,
    load_sem, hop_load, halo_send, halo_recv, forward_send, forward_recv, core_send, core_recv, plane_send, plane_recv,
    depth_send, depth_recv, gather_send, gather_recv, pass_send, pass_recv,
    ncore_sem, nplane_send, nplane_recv, ndepth_send, ndepth_recv,
):
    site, mode = lax.axis_index("site"), lax.axis_index("mode")
    y, z, x_lo = site % 4, (site // 4) % 8, site // 32
    core, x_hi = mode % 2, mode // 2
    x = x_hi * 2 + x_lo
    slot = x * 4 + y
    t, r = site // 8, site % 8

    def device(px, py, pz, pc):
        return ((px % 2) * 32 + pz * 4 + py, (px // 2) * 2 + pc)

    other = (site, x_hi * 2 + 1 - core)
    far = (mode + 2) % 4
    mate, far_mate = other[1], (other[1] + 2) % 4
    plane = [((x + dx) % 4, (y + dy) % 4) for dx, dy in PLANE]
    deep = [(z + d) % 8 for d in DEPTH]
    sites = {
        1: t * 8 + (r + 4) % 8,
        2: t * 8 + r // 4 * 4 + (r % 4 + 2) % 4,
        3: t * 8 + r // 2 * 2 + (r + 1) % 2,
        4: ((t + 7) % 8) * 8 + r,
        5: ((t + 1) % 8) * 8 + r,
    }

    barrier = pltpu.get_barrier_semaphore()
    greeted = [other] + [device(px, py, z, core) for px, py in plane] + [device(x, y, pz, c) for pz in deep for c in (core, 1 - core)]
    greeted += [(sites[k], mode) for k in (4, 5)]
    for peer in greeted:
        pl.semaphore_signal(barrier, inc=1, device_id=peer, device_id_type=MESH)

    loads = [
        pltpu.make_async_copy(src, dst, load_sem.at[n])
        for n, (src, dst) in enumerate(((basis, a_v), (images, i_v), (rotation, r_v), (neighbours, nb_s)))
    ]
    for copy in loads:
        copy.start()

    def remote(src, dst, send_sem, recv_sem, peer):
        copy = pltpu.make_async_remote_copy(
            src_ref=src, dst_ref=dst, send_sem=send_sem, recv_sem=recv_sem, device_id=peer, device_id_type=MESH
        )
        return copy

    def arrived(dst, send_sem, recv_sem):
        remote(dst, dst, send_sem, recv_sem, other).wait_recv()

    loads[0].wait()
    spread = (
        (iota((128, 128), 0) - 112 == iota((128, 128), 1) % 16) & (iota((128, 128), 0) >= 112)
    ).astype(F32).astype(BF16)
    own_lanes = iota((800, 128), 0) % 8 == iota((800, 128), 1) // 16
    repeated = dot(a_v[:, 384:512], spread, 1, 0)
    repeated = jnp.where(own_lanes, repeated, 0.0).astype(BF16)
    put = (iota((800, 128), 0) // 8 + 100 * mode) % 128 == iota((800, 128), 1)
    piece[0, mode] = dot(repeated, put.astype(F32).astype(BF16), 0, 0).astype(BF16)

    loads[1].wait()
    hop_loads = [pltpu.make_async_copy(hops.at[h], h_v.at[h], hop_load.at[h]) for h in range(9)]
    for copy in hop_loads:
        copy.start()
    part[:, 0:384] = dot(a_v[...], i_v[:, 0:384], 0, 0)
    part[:, 384:496] = dot(a_v[...], i_v[:, 384:496], 0, 0)
    part[:, 496:512] = jnp.zeros((512, 16), F32)

    pl.semaphore_wait(barrier, len(greeted))

    sent = []

    def start(copy):
        copy.start()
        sent.append(copy)

    mine = piece.at[0, mode]
    for k, m in ((0, far), (4, mode), (5, mode), (2, mode), (1, mode), (3, mode)):
        target = site if k == 0 else sites[k]
        start(remote(mine, piece.at[k, mode], halo_send.at[k, m // 2], halo_recv.at[k, mode // 2], (target, m)))
    start(remote(mine, piece.at[0, mode], forward_send.at[0, x_hi], forward_recv.at[0, x_hi], other))
    columns = [(x + dx) % 4 for dx in AWAY]

    def quarter(c, px):
        return pl.ds(pl.multiple_of(256 * c + 64 * px, 64), 64)

    for n, px in enumerate(columns):
        start(remote(part.at[quarter(1 - core, px)], core_in.at[px], core_send.at[n], core_recv.at[n], other))

    loads[2].wait()
    basis_out[...] = dot(a_v[...], r_v[...], 1, 0).astype(BF16)

    for n, px in enumerate(columns):
        arrived(core_in.at[px], core_send.at[n], core_recv.at[n])
        summed = part[quarter(core, px), :] + core_in[px]
        for q in range(4):
            half[4 * px + q] = summed[16 * q : 16 * q + 16]
            plane_out[4 * px + q] = summed[16 * q : 16 * q + 16].astype(BF16)
        for dy in AWAY:
            if AWAY[n] or dy:
                py, k = (y + dy) % 4, PLANE.index((AWAY[n], dy))
                start(remote(plane_out.at[4 * px + py], plane_in.at[k], plane_send.at[k], plane_recv.at[k], device(px, py, z, core)))

    arrived(piece.at[0, far], halo_send.at[0, far // 2], halo_recv.at[0, far // 2])
    for k in (4, 5, 2, 1, 3):
        start(remote(piece.at[0, far], piece.at[k, far], halo_send.at[k, 1 - x_hi], halo_recv.at[k, far // 2], (sites[k], mode)))
    start(remote(piece.at[0, far], piece.at[0, far], forward_send.at[0, far // 2], forward_recv.at[0, far // 2], other))

    rot_part[...] = dot(i_v[...], r_v[0:496, :], 1, 0)

    lane = iota((8, 16, 128), 2)

    def forward(where):
        for k, m in where:
            arrived(piece.at[k, m], halo_send.at[k, m // 2], halo_recv.at[k, m // 2])
            start(remote(piece.at[k, m], piece.at[k, m], forward_send.at[k, m // 2], forward_recv.at[k, m // 2], other))

    def widen(groups):
        for k in groups:
            for m in (mate, far_mate):
                arrived(piece.at[k, m], forward_send.at[k, m // 2], forward_recv.at[k, m // 2])
            p0, p1, p2, p3 = (piece[k, m].reshape(8, 16, 128) for m in range(4))
            rows = pl.ds(8 * k, 8)
            wide[rows, :, 0:128] = jnp.where(lane < 100, p0, p1)
            wide[rows, :, 128:256] = jnp.where(lane < 72, p1, p2)
            wide[rows, :, 256:384] = jnp.where(lane < 44, p2, p3)
            wide[rows, :, 384:512] = p3

    def gather_rows(h):
        for b in range(8):
            e = b if h == 0 else nb_s[b, h - 1]
            gath[h, 16 * b : 16 * b + 16, :] = wide[e]

    def stencil(hs):
        for h in hs:
            gather_rows(h)
            hop_loads[h].wait()
        for c in range(5):
            rows = pl.ds(160 * c, 160)
            term = None if hs[0] == 0 else image_sum[rows, :]
            for h in hs:
                product = dot(h_v[h, rows, :], gath[h, :, 0:400], 1, 1)
                term = product if term is None else term + product
            image_sum[rows, :] = term

    forward(((3, mode), (1, mode), (2, mode), (4, mode), (5, mode), (3, far), (1, far), (2, far), (4, far), (5, far)))
    for n in range(15):
        arrived(plane_in.at[n], plane_send.at[n], plane_recv.at[n])
    total = half[slot]
    for n in range(15):
        total = total + plane_in[n].astype(F32)
    depth_buf[z] = total
    for n, pz in enumerate(deep):
        start(remote(depth_buf.at[z], depth_buf.at[z], depth_send.at[n], depth_recv.at[z], device(x, y, pz, core)))

    widen((0, 1, 2, 3))
    loads[3].wait()
    stencil((0, 1, 2, 3))
    stencil((4, 5, 6))

    widen((4, 5))
    stencil((7, 8))
    image = jnp.where(own_lanes, image_sum[...], 0.0).astype(BF16)

    by_block = dot(image, a_v[...], 0, 0)
    new = by_block[0:16]
    for b in range(1, 8):
        new = new + by_block[16 * b : 16 * b + 16]
    new_part[0] = new[:, 0:256]
    new_part[1] = new[:, 256:512]
    start(remote(new_part.at[1 - core], new_core, ncore_sem.at[0], ncore_sem.at[1], other))

    last = jnp.concatenate([r_v[496:512, :]] * 8, axis=0)
    images_out[...] = (rot_part[...] + dot(image, last, 1, 0)).astype(BF16)

    arrived(new_core, ncore_sem.at[0], ncore_sem.at[1])
    new_plane[slot] = (new_part[core] + new_core[...]).astype(BF16)
    for n, (px, py) in enumerate(plane):
        start(remote(new_plane.at[slot], new_plane.at[slot], nplane_send.at[n], nplane_recv.at[slot], device(px, py, z, core)))

    for pz in deep:
        arrived(depth_buf.at[pz], depth_send.at[0], depth_recv.at[pz])
    total = depth_buf[0]
    for n in range(1, 8):
        total = total + depth_buf[n]
    gathered[16 * core + slot] = (total * scale).astype(BF16)
    own = gathered.at[16 * core + slot]
    for n, (px, py) in enumerate(plane):
        start(remote(own, own, gather_send.at[n], gather_recv.at[slot], device(px, py, z, core)))
    start(remote(own, own, pass_send.at[slot], pass_recv.at[slot], other))

    for px, py in plane:
        q = 4 * px + py
        arrived(new_plane.at[q], nplane_send.at[0], nplane_recv.at[q])
    total = new_plane[0].astype(F32)
    for n in range(1, 16):
        total = total + new_plane[n].astype(F32)
    new_depth[core, z] = total.astype(BF16)
    own = new_depth.at[core, z]
    for n, pz in enumerate(deep):
        for c in (core, 1 - core):
            start(remote(own, own, ndepth_send.at[n, c], ndepth_recv.at[core, z], device(x, y, pz, c)))
    start(remote(own, own, ndepth_send.at[7, 0], ndepth_recv.at[core, z], other))

    def put_out(q):
        proj_out[pl.ds(pl.multiple_of(16 * q, 16), 16), :] = gathered[q].astype(F32)

    put_out(16 * core + slot)
    for px, py in plane[::-1]:
        q = 4 * px + py
        block = gathered.at[16 * core + q]
        arrived(block, gather_send.at[0], gather_recv.at[q])
        start(remote(block, block, pass_send.at[q], pass_recv.at[q], other))
        put_out(16 * core + q)
    for q in range(16):
        arrived(gathered.at[16 * (1 - core) + q], pass_send.at[0], pass_recv.at[q])
        put_out(16 * (1 - core) + q)

    for pz in deep:
        arrived(new_depth.at[core, pz], ndepth_send.at[0, 0], ndepth_recv.at[core, pz])
    for pz in [z] + deep:
        arrived(new_depth.at[1 - core, pz], ndepth_send.at[0, 0], ndepth_recv.at[1 - core, pz])
    for c in range(2):
        total = new_depth[c, 0].astype(F32)
        for n in range(1, 8):
            total = total + new_depth[c, n].astype(F32)
        proj_out[256 * c : 256 * c + 256, 496:512] = (total * scale).T

    for copy in sent:
        copy.wait_send()


def finish(*refs):
    copies = [pltpu.make_async_copy(refs[n], refs[3 + n], refs[6].at[n]) for n in range(3)]
    for copy in copies:
        copy.start()
    for copy in copies:
        copy.wait()


def local(basis, images, hops, neighbours, rotation):
    blocks, modes, nvec = basis.shape
    old = images.shape[2]
    rows = blocks * modes
    sites = lax.axis_size("site") * lax.axis_size("mode")
    scale = 1.0 / math.sqrt(rows * sites)
    flat = lambda v: jnp.transpose(v, (1, 0, 2)).reshape(rows, v.shape[2])
    by_hop = jnp.transpose(hops, (1, 2, 0, 3)).reshape(9, rows, hops.shape[3])
    hbm = pl.BlockSpec(memory_space=pltpu.HBM)
    vmem = pl.BlockSpec(memory_space=pltpu.VMEM)
    dma = pltpu.SemaphoreType.DMA
    projected, rotated_basis, rotated_images = pl.pallas_call(
        functools.partial(kernel, scale),
        out_shape=(
            pltpu.VMEM((nvec, nvec), F32),
            pltpu.VMEM((rows, nvec), BF16),
            pltpu.VMEM((rows, nvec), BF16),
        ),
        in_specs=[hbm] * 5,
        out_specs=(vmem, vmem, vmem),
        scratch_shapes=[
            pltpu.VMEM((rows, nvec), BF16),
            pltpu.VMEM((rows, old), BF16),
            pltpu.VMEM(by_hop.shape, BF16),
            pltpu.VMEM((nvec, nvec), BF16),
            pltpu.SMEM((8, 8), jnp.int32),
            pltpu.VMEM((6, 4, 128, 128), BF16),
            pltpu.VMEM((48, 16, 512), BF16),
            pltpu.VMEM((9, 128, 512), BF16),
            pltpu.VMEM((512, 512), F32),
            pltpu.VMEM((rows, 128), F32),
            pltpu.VMEM((4, 64, 512), F32),
            pltpu.VMEM((16, 16, 512), F32),
            pltpu.VMEM((16, 16, 512), BF16),
            pltpu.VMEM((15, 16, 512), BF16),
            pltpu.VMEM((8, 16, 512), F32),
            pltpu.VMEM((32, 16, 512), BF16),
            pltpu.VMEM((rows, nvec), F32),
            pltpu.VMEM((2, 16, 256), F32),
            pltpu.VMEM((16, 256), F32),
            pltpu.VMEM((16, 16, 256), BF16),
            pltpu.VMEM((2, 8, 16, 256), BF16),
            dma((4,)),
            dma((9,)),
            dma((6, 2)),
            dma((6, 2)),
            dma((6, 2)),
            dma((6, 2)),
            dma((4,)),
            dma((4,)),
            dma((15,)),
            dma((15,)),
            dma((7,)),
            dma((8,)),
            dma((15,)),
            dma((16,)),
            dma((16,)),
            dma((16,)),
            dma((2,)),
            dma((15,)),
            dma((16,)),
            dma((8, 2)),
            dma((2, 8)),
        ],
        compiler_params=pltpu.CompilerParams(
            collective_id=0, has_side_effects=True, vmem_limit_bytes=40 * 2**20
        ),
    )(*(pltpu.with_memory_space_constraint(v, pltpu.HBM) for v in (flat(basis), flat(images), by_hop, neighbours, rotation)))
    projected, rotated_basis, rotated_images = pl.pallas_call(
        finish,
        out_shape=(
            jax.ShapeDtypeStruct((nvec, nvec), F32),
            jax.ShapeDtypeStruct((rows, nvec), BF16),
            jax.ShapeDtypeStruct((rows, nvec), BF16),
        ),
        in_specs=[pl.BlockSpec(memory_space=pl.ANY)] * 3,
        out_specs=(hbm, hbm, hbm),
        scratch_shapes=[dma((3,))],
        compiler_params=pltpu.CompilerParams(vmem_limit_bytes=2**20),
    )(projected, rotated_basis, rotated_images)
    unflat = lambda v: jnp.transpose(v.reshape(modes, blocks, nvec), (1, 0, 2))
    return projected, unflat(rotated_basis), unflat(rotated_images)


def solution(mesh):
    placed = (
        P("site", "mode", None),
        P("site", "mode", None),
        P("site", None, "mode", None),
        P("site", None),
        P(),
    )
    return jax.shard_map(
        local,
        mesh=mesh,
        in_specs=placed,
        out_specs=(P(), P("site", "mode", None), P("site", "mode", None)),
        check_vma=False,
    )
```
